32 devices in a mesh: row: 16 (over z, y, core), col: 2 (over x).
Axes of the slice: x: 2, y: 2, z: 4, core: 2. Of those that a mesh axis runs over, the one named last changes fastest.
Arguments:
- fine_matrix: bfloat16 [4096, 1536], P('row', 'col'), may hold values from -0.75 to 0.75
- fine_columns: int32 [64, 24], P('row'), may hold values from 0 to 63, as said below
- fine_counts: int32 [64], P('row'), may hold values from 12 to 24, as said below
- prolong: bfloat16 [4096, 128], P('row'), may hold values from -6 to 6
- prolong_columns: int32 [64, 2], P('row'), may hold values from 0 to 31
- restrict_rows: bfloat16 [2048, 256], P('row'), may hold values from -0.375 to 0.375
- coarse_pattern: int32 [16, 48], P('row'), may hold values from -1 to 31, as said below
Outputs:
- coarse_operator: float32 [2048, 3072], P('row', 'col')
The draws below stay inside these ranges and needn't reach their ends.
Inputs may be any that keep to these rules, and one draw needn't show every extreme that they name: Only the first fine_counts[i] block slots of fine brick i are live. `fine_columns`: at most 4 block slots of each fine brick couple to a brick more than 8 bricks away, counting cyclically over the 64 bricks. `coarse_pattern`: each row holds distinct coarse brick numbers and -1 in slots left empty; every coarse brick reached by a live product of the slab is listed.
All inputs are finite; a program needn't handle non-finite values.
Results may differ from the reference program's by a relative error of at most 0.00035.
Values may be sent and summed in bfloat16 or wider, within the bound.
No kernel may reach another device: no remote copies, remote signals or barrier semaphores. Data moves between devices by JAX's collectives and lax.ppermute only.
A program may use at most 64 MiB of HBM per device.

```python
import jax
import jax.numpy as jnp
from jax import lax

BRICK = 64
SLAB_BRICKS = 4
A_SLOTS = 24
P_SLOTS = 2
NEAR = 8
FAR_SLOTS = 4
SLABS = 16
FINE = 64
COARSE = 32
PATTERN = 48
PATTERN_OWN = 24


def layout(key):
    near_key = jax.random.fold_in(key, 11)
    far_key = jax.random.fold_in(key, 23)
    order_key = jax.random.fold_in(key, 37)
    count_key = jax.random.fold_in(key, 41)
    side_key = jax.random.fold_in(key, 53)
    rows = jnp.arange(FINE, dtype=jnp.int32)
    offsets = jax.random.randint(near_key, (FINE, A_SLOTS), -NEAR, NEAR + 1, dtype=jnp.int32)
    distant = jax.random.randint(far_key, (FINE, A_SLOTS), 0, FINE, dtype=jnp.int32)
    scores = jax.random.randint(order_key, (FINE, A_SLOTS), 0, 1 << 20, dtype=jnp.int32) * A_SLOTS
    scores = scores + jnp.arange(A_SLOTS, dtype=jnp.int32)[None, :]
    ranks = jnp.argsort(jnp.argsort(scores, axis=1), axis=1)
    columns = jnp.where(ranks < FAR_SLOTS, distant, (rows[:, None] + offsets) % FINE).astype(jnp.int32)
    counts = jax.random.randint(count_key, (FINE,), A_SLOTS // 2, A_SLOTS + 1, dtype=jnp.int32)
    counts = counts.at[0].set(A_SLOTS)
    side = jax.random.randint(side_key, (FINE,), 0, 2, dtype=jnp.int32) * 2 - 1
    parent = rows // 2
    targets = jnp.stack([parent, (parent + side) % COARSE], axis=1).astype(jnp.int32)
    reached = targets[columns]
    live_slots = jnp.arange(A_SLOTS, dtype=jnp.int32)[None, :] < counts[:, None]
    values = jnp.where(live_slots[:, :, None], reached, COARSE).reshape(SLABS, SLAB_BRICKS * A_SLOTS * 2)
    ordered = jnp.sort(values, axis=1)
    repeat = ordered[:, 1:] == ordered[:, :-1]
    cleaned = jnp.concatenate([ordered[:, :1], jnp.where(repeat, COARSE, ordered[:, 1:])], axis=1)
    distinct = jnp.sort(cleaned, axis=1)[:, :PATTERN]
    distinct = jnp.where(distinct == COARSE, -1, distinct)
    owners = PATTERN // PATTERN_OWN
    pattern = distinct.reshape(SLABS, PATTERN_OWN, owners).transpose(0, 2, 1).reshape(SLABS, PATTERN)
    return (columns, counts, targets, pattern.astype(jnp.int32))


def draw_fine_columns(key, part):
    return layout(key)[0]


def draw_fine_counts(key, part):
    return layout(key)[1]


def draw_prolong_columns(key, part):
    return layout(key)[2]


def draw_coarse_pattern(key, part):
    return layout(key)[3]


def steps_of(rng, shape, cuts, least, high):
    factor_of, own = 1.0, jax.random.fold_in(rng, 6)
    for axis_at, shards_of in cuts:
        steps = jnp.exp(jax.random.uniform(jax.random.fold_in(own, axis_at), (shards_of,), jnp.float32, least / len(cuts), high / len(cuts)))
        factor_of = factor_of * jnp.repeat(steps, shape[axis_at] // shards_of).reshape([-1 if axis == axis_at else 1 for axis in range(len(shape))])
    return factor_of


def bell_draw(own_key, dims, deviation, most, cuts=(), kind=jnp.bfloat16):
    values = deviation * jax.random.normal(own_key, dims, jnp.float32)
    if cuts:
        values = values * steps_of(own_key, dims, cuts, -0.22, 0.18)
    return jnp.clip(values, -most, most).astype(kind)


def setup_inputs(seed: int = 0) -> dict:
    splits = jax.random.split(jax.random.key(seed), 8)
    fine_matrix = bell_draw(splits[0], (FINE * BRICK, A_SLOTS * BRICK), BRICK ** -0.5, 0.75, ((0, 16), (1, 2)))
    fine_columns = draw_fine_columns(jax.random.fold_in(splits[7], 71), 0)
    fine_counts = draw_fine_counts(jax.random.fold_in(splits[7], 71), 0)
    prolong = bell_draw(splits[3], (FINE * BRICK, P_SLOTS * BRICK), 1.0, 6.0, ((0, 16),))
    prolong_columns = draw_prolong_columns(jax.random.fold_in(splits[7], 71), 0)
    restrict_rows = bell_draw(splits[5], (COARSE * BRICK, SLAB_BRICKS * BRICK), (SLAB_BRICKS * BRICK) ** -0.5, 0.375, ((0, 16),))
    coarse_pattern = draw_coarse_pattern(jax.random.fold_in(splits[7], 71), 0)
    return dict(fine_matrix=fine_matrix, fine_columns=fine_columns, fine_counts=fine_counts, prolong=prolong, prolong_columns=prolong_columns, restrict_rows=restrict_rows, coarse_pattern=coarse_pattern)


def reference(fine_matrix, fine_columns, fine_counts, prolong, prolong_columns, restrict_rows, coarse_pattern):
    blocks = prolong.reshape(FINE, BRICK, P_SLOTS * BRICK)
    coarse_rows = (SLAB_BRICKS // 2) * BRICK

    def one_slab(slab_index):
        first_row = (slab_index * SLAB_BRICKS).astype(jnp.int32)
        columns = lax.dynamic_slice_in_dim(fine_columns, first_row, SLAB_BRICKS, 0)
        counts = lax.dynamic_slice_in_dim(fine_counts, first_row, SLAB_BRICKS, 0)
        a_rows = lax.dynamic_slice_in_dim(fine_matrix, (first_row * BRICK).astype(jnp.int32), SLAB_BRICKS * BRICK, 0)
        r_rows = lax.dynamic_slice_in_dim(restrict_rows, (slab_index * coarse_rows).astype(jnp.int32), coarse_rows, 0)
        pattern = lax.dynamic_slice_in_dim(coarse_pattern, slab_index.astype(jnp.int32), 1, 0)[0]
        chosen = jnp.take(blocks, columns, axis=0)
        reached = jnp.take(prolong_columns, columns, axis=0)
        live_slots = jnp.arange(A_SLOTS, dtype=jnp.int32)[None, :] < counts[:, None]
        a_blocks = a_rows.reshape(SLAB_BRICKS, BRICK, A_SLOTS, BRICK).astype(jnp.float32)
        products = jnp.einsum('iakb,ikbc->ikac', a_blocks, chosen.astype(jnp.float32), precision=lax.Precision.HIGHEST)
        products = products.reshape(SLAB_BRICKS, A_SLOTS, BRICK, P_SLOTS, BRICK)
        matches = ((reached[:, :, :, None] == pattern[None, None, None, :]) & live_slots[:, :, None, None]).astype(jnp.float32)
        partial_value = jnp.einsum('ikqs,ikaqc->iasc', matches, products, precision=lax.Precision.HIGHEST)
        partial_value = partial_value.reshape(SLAB_BRICKS * BRICK, PATTERN * BRICK)
        return jnp.dot(r_rows.astype(jnp.float32), partial_value, precision=lax.Precision.HIGHEST)

    stacked = lax.map(one_slab, jnp.arange(SLABS, dtype=jnp.int32))
    return stacked.reshape(SLABS * coarse_rows, PATTERN * BRICK)
```

```python
import functools

import jax
import jax.numpy as jnp
from jax import lax
from jax.experimental import pallas as pl
from jax.experimental.pallas import tpu as pltpu
from jax.sharding import PartitionSpec as P

BRICK = 64
P_SLOTS = 2
DIGIT = 128
LANES = 128
EXTRA = 16


def pack_kernel(columns_ref, prolong_ref, packed_ref):
    rows = prolong_ref.shape[0]
    packed_ref[:rows, :] = prolong_ref[...]
    row = lax.broadcasted_iota(jnp.int32, (EXTRA, LANES), 0)
    lane = lax.broadcasted_iota(jnp.int32, (EXTRA, LANES), 1)
    digits = jnp.zeros((EXTRA, LANES), jnp.int32)
    for brick in range(columns_ref.shape[0]):
        for q in range(P_SLOTS):
            value = columns_ref[brick, q]
            here = lane == brick * P_SLOTS + q
            digits = jnp.where(here & (row == 0), value % DIGIT, digits)
            digits = jnp.where(here & (row == 1), value // DIGIT, digits)
    packed_ref[rows:, :] = digits.astype(jnp.float32).astype(jnp.bfloat16)


def pack(prolong, prolong_columns):
    return pl.pallas_call(
        pack_kernel,
        out_shape=jax.ShapeDtypeStruct((prolong.shape[0] + EXTRA, LANES), jnp.bfloat16),
        in_specs=[
            pl.BlockSpec(memory_space=pltpu.SMEM),
            pl.BlockSpec(memory_space=pltpu.VMEM),
        ],
        out_specs=pl.BlockSpec(memory_space=pltpu.VMEM),
        name="pack",
    )(prolong_columns, prolong)


def swap(block, axis, size, mask):
    return lax.ppermute(block, axis, [(i, i ^ mask) for i in range(size)])


def gather_row(packed, size):
    if size & (size - 1) or size < 8 or size > 32:
        return [lax.all_gather(packed, "row", axis=0, tiled=True)], False
    pieces = {0: packed}
    for mask in (8, 12, 4, 16, 20, 24, 28):
        if mask < size:
            pieces[mask] = swap(packed, "row", size, mask)
    for mask in sorted(pieces):
        pieces[mask | 2] = swap(pieces[mask], "row", size, 2)
    for mask in sorted(pieces):
        pieces[mask | 1] = swap(pieces[mask], "row", size, 1)
    return [pieces[mask] for mask in range(size)], True


def operator_kernel(
    slabs, by_xor, columns_ref, counts_ref, pattern_ref, restrict_ref, *refs, cols, parts
):
    fines = refs[:cols]
    pieces = refs[cols : cols + parts]
    out_ref, held_ref, seen_ref, reached_ref, slot_ref, sums_ref, sem = refs[cols + parts :]
    bricks, slots = columns_ref.shape
    share = slots // cols
    owned = pattern_ref.shape[1] // cols
    rows = bricks * BRICK + EXTRA
    row_index = lax.axis_index("row")
    col_index = lax.axis_index("col")

    if parts > 1:
        for at, piece in enumerate(pieces):
            held_ref[at * rows : (at + 1) * rows, :] = piece[...]
        source = held_ref
    else:
        source = pieces[0]
    for at in range(slabs):
        first = at * rows + bricks * BRICK
        digits = source[first : first + EXTRA, :].astype(jnp.float32)
        seen_ref[at : at + 1, :] = (digits[0:1, :] + DIGIT * digits[1:2, :]).astype(jnp.int32)
    move = pltpu.make_async_copy(seen_ref, reached_ref, sem)
    move.start()

    owned_first = col_index * owned
    for s in range(owned * cols):
        mine = s - owned_first
        mine = jnp.where((mine >= 0) & (mine < owned), mine, owned)
        slot_ref[pattern_ref[0, s] + 1] = mine
    sums_ref[...] = jnp.zeros_like(sums_ref)
    left = lax.broadcasted_iota(jnp.int32, (BRICK, LANES), 1) < BRICK
    nothing = jnp.zeros((BRICK, LANES), jnp.bfloat16)
    move.wait()

    for i in range(bricks):
        for part in range(cols):
            part_first = (col_index ^ part) * share if cols > 1 else 0
            for pair in range(share // 2):
                blocks, where_to = [], []
                for half in range(2):
                    k = part_first + pair * 2 + half
                    brick = columns_ref[i, k]
                    slab = lax.div(brick, bricks)
                    inner = brick - slab * bricks
                    if by_xor:
                        slab = slab ^ row_index
                    start = pl.multiple_of(slab * rows + inner * BRICK, 16)
                    blocks.append(source[pl.ds(start, BRICK), :])
                    live = k < counts_ref[i]
                    for q in range(P_SLOTS):
                        coarse = reached_ref[slab, inner * P_SLOTS + q]
                        where_to.append(jnp.where(live, slot_ref[coarse + 1], owned))
                right = jnp.concatenate(
                    [
                        jnp.concatenate([blocks[0], nothing], axis=1),
                        jnp.concatenate([nothing, blocks[1]], axis=1),
                    ],
                    axis=0,
                )
                a = fines[part][i * BRICK : (i + 1) * BRICK, pair * LANES : (pair + 1) * LANES]
                product = jnp.dot(a, right, preferred_element_type=jnp.float32)
                for half in range(2):
                    block = product[:, half * LANES : (half + 1) * LANES]
                    sums_ref[i, where_to[half * 2]] += jnp.where(left, block, 0.0)
                    sums_ref[i, where_to[half * 2 + 1]] += jnp.where(left, 0.0, block)

    restrict = restrict_ref[...]
    for pair in range(owned // 2):
        high, low = [], []
        for i in range(bricks):
            even, odd = sums_ref[i, 2 * pair], sums_ref[i, 2 * pair + 1]
            total = jnp.where(left, even, odd) + pltpu.roll(
                jnp.where(left, odd, even), BRICK, 1
            )
            top = total.astype(jnp.bfloat16)
            high.append(top)
            low.append((total - top.astype(jnp.float32)).astype(jnp.bfloat16))
        high = jnp.concatenate(high, axis=0)
        low = jnp.concatenate(low, axis=0)
        out_ref[:, pair * LANES : (pair + 1) * LANES] = jnp.dot(
            restrict, high, preferred_element_type=jnp.float32
        ) + jnp.dot(restrict, low, preferred_element_type=jnp.float32)


def local(
    slabs,
    cols,
    fine_matrix,
    fine_columns,
    fine_counts,
    prolong,
    prolong_columns,
    restrict_rows,
    coarse_pattern,
):
    bricks = fine_counts.shape[0]
    owned = coarse_pattern.shape[1] // cols
    coarse = restrict_rows.shape[0] // BRICK * slabs
    packed = pack(prolong, prolong_columns)
    pieces, by_xor = gather_row(packed, slabs)
    fines = [fine_matrix] + [swap(fine_matrix, "col", cols, d) for d in range(1, cols)]
    rows = packed.shape[0]
    smem = pl.BlockSpec(memory_space=pltpu.SMEM)
    vmem = pl.BlockSpec(memory_space=pltpu.VMEM)
    held_rows = slabs * rows if len(pieces) > 1 else 16
    return pl.pallas_call(
        functools.partial(operator_kernel, slabs, by_xor, cols=cols, parts=len(pieces)),
        out_shape=jax.ShapeDtypeStruct((restrict_rows.shape[0], owned * BRICK), jnp.float32),
        in_specs=[smem] * 3 + [vmem] * (1 + cols + len(pieces)),
        out_specs=vmem,
        scratch_shapes=[
            pltpu.VMEM((held_rows, LANES), jnp.bfloat16),
            pltpu.VMEM((slabs, LANES), jnp.int32),
            pltpu.SMEM((slabs, LANES), jnp.int32),
            pltpu.SMEM((coarse + 1,), jnp.int32),
            pltpu.VMEM((bricks, owned + 1, BRICK, LANES), jnp.float32),
            pltpu.SemaphoreType.DMA,
        ],
        compiler_params=pltpu.CompilerParams(vmem_limit_bytes=32 * 1024 * 1024),
        name="operator",
    )(fine_columns, fine_counts, coarse_pattern, restrict_rows, *fines, *pieces)


def solution(mesh):
    return jax.shard_map(
        functools.partial(local, mesh.shape["row"], mesh.shape["col"]),
        mesh=mesh,
        in_specs=(
            P("row", "col"),
            P("row", None),
            P("row"),
            P("row", None),
            P("row", None),
            P("row", None),
            P("row", None),
        ),
        out_specs=P("row", "col"),
        check_vma=False,
    )
```

```python
import functools

import jax
import jax.numpy as jnp
from jax import lax
from jax.experimental import pallas as pl
from jax.experimental.pallas import tpu as pltpu
from jax.sharding import PartitionSpec as P

BRICK = 64
P_SLOTS = 2
DIGIT = 128
LANES = 128
EXTRA = 16


def pack_kernel(columns_ref, prolong_ref, packed_ref):
    rows = prolong_ref.shape[0]
    packed_ref[:rows, :] = prolong_ref[...]
    row = lax.broadcasted_iota(jnp.int32, (EXTRA, LANES), 0)
    lane = lax.broadcasted_iota(jnp.int32, (EXTRA, LANES), 1)
    digits = jnp.zeros((EXTRA, LANES), jnp.int32)
    for brick in range(columns_ref.shape[1]):
        for q in range(P_SLOTS):
            value = columns_ref[q, brick]
            here = lane == brick * P_SLOTS + q
            digits = jnp.where(here & (row == 0), value % DIGIT, digits)
            digits = jnp.where(here & (row == 1), value // DIGIT, digits)
    packed_ref[rows:, :] = digits.astype(jnp.float32).astype(jnp.bfloat16)


def pack(prolong, prolong_columns):
    return pl.pallas_call(
        pack_kernel,
        out_shape=pltpu.VMEM((prolong.shape[0] + EXTRA, LANES), jnp.bfloat16),
        in_specs=[
            pl.BlockSpec(memory_space=pltpu.SMEM),
            pl.BlockSpec(memory_space=pltpu.VMEM),
        ],
        out_specs=pl.BlockSpec(memory_space=pltpu.VMEM),
        name="pack",
    )(prolong_columns.T, prolong)


def swap(block, axis, size, mask):
    return lax.ppermute(block, axis, [(i, i ^ mask) for i in range(size)])


def gather_row(packed, size, fine_other):
    if size != 16:
        return [lax.all_gather(packed, "row", axis=0, tiled=True)], None, fine_other
    got = {0: packed}
    for mask, source, hop in (
        (2, 0, 2),
        (8, 0, 8),
        (12, 0, 12),
        (4, 0, 4),
        (6, 2, 4),
        (10, 8, 2),
        (14, 12, 2),
    ):
        got[mask] = swap(got[source], "row", size, hop)
    arrays, masks = list(got.values()), [[mask] for mask in got]
    for group in ((0, 2, 4, 6), (8, 12), (10, 14)):
        both = jnp.concatenate([got[mask] for mask in group])
        if group[0] == 10:
            both, fine_other = lax.optimization_barrier((both, fine_other))
        arrays.append(swap(both, "row", size, 1))
        masks.append([mask | 1 for mask in group])
    return arrays, masks, fine_other


def operator_kernel(
    slabs, masks, columns_ref, counts_ref, pattern_ref, restrict_ref, *refs, cols
):
    parts = len(masks) if masks else 1
    fines = refs[:cols]
    pieces = refs[cols : cols + parts]
    out_ref, held_ref, seen_ref, reached_ref, slot_ref, sums_ref, sem = refs[cols + parts :]
    bricks, slots = columns_ref.shape
    share = slots // cols
    owned = pattern_ref.shape[1] // cols
    rows = bricks * BRICK + EXTRA
    row_index = lax.axis_index("row")
    col_index = lax.axis_index("col")

    if parts > 1:
        for piece, inside in zip(pieces, masks):
            for at, mask in enumerate(inside):
                held_ref[mask * rows : (mask + 1) * rows, :] = piece[at * rows : (at + 1) * rows, :]
        source = held_ref
    else:
        source = pieces[0]
    for at in range(slabs):
        first = at * rows + bricks * BRICK
        digits = source[first : first + EXTRA, :].astype(jnp.float32)
        seen_ref[at : at + 1, :] = (digits[0:1, :] + DIGIT * digits[1:2, :]).astype(jnp.int32)
    move = pltpu.make_async_copy(seen_ref, reached_ref, sem)
    move.start()

    owned_first = col_index * owned
    for s in range(owned * cols):
        mine = s - owned_first
        mine = jnp.where((mine >= 0) & (mine < owned), mine, owned)
        slot_ref[pattern_ref[0, s] + 1] = mine
    sums_ref[...] = jnp.zeros_like(sums_ref)
    left = lax.broadcasted_iota(jnp.int32, (BRICK, LANES), 1) < BRICK
    nothing = jnp.zeros((BRICK, LANES), jnp.bfloat16)
    move.wait()

    for i in range(bricks):
        for part in range(cols):
            part_first = (col_index ^ part) * share if cols > 1 else 0
            for pair in range(share // 2):
                blocks, where_to = [], []
                for half in range(2):
                    k = part_first + pair * 2 + half
                    brick = columns_ref[i, k]
                    slab = lax.div(brick, bricks)
                    inner = brick - slab * bricks
                    if masks:
                        slab = slab ^ row_index
                    start = pl.multiple_of(slab * rows + inner * BRICK, 16)
                    blocks.append(source[pl.ds(start, BRICK), :])
                    live = k < counts_ref[i]
                    for q in range(P_SLOTS):
                        coarse = reached_ref[slab, inner * P_SLOTS + q]
                        where_to.append(jnp.where(live, slot_ref[coarse + 1], owned))
                right = jnp.concatenate(
                    [
                        jnp.concatenate([blocks[0], nothing], axis=1),
                        jnp.concatenate([nothing, blocks[1]], axis=1),
                    ],
                    axis=0,
                )
                a = fines[part][i * BRICK : (i + 1) * BRICK, pair * LANES : (pair + 1) * LANES]
                product = jnp.dot(a, right, preferred_element_type=jnp.float32)
                for half in range(2):
                    block = product[:, half * LANES : (half + 1) * LANES]
                    sums_ref[i, where_to[half * 2]] += jnp.where(left, block, 0.0)
                    sums_ref[i, where_to[half * 2 + 1]] += jnp.where(left, 0.0, block)

    restrict = restrict_ref[...]
    for pair in range(owned // 2):
        high, low = [], []
        for i in range(bricks):
            even, odd = sums_ref[i, 2 * pair], sums_ref[i, 2 * pair + 1]
            total = jnp.where(left, even, odd) + pltpu.roll(
                jnp.where(left, odd, even), BRICK, 1
            )
            top = total.astype(jnp.bfloat16)
            high.append(top)
            low.append((total - top.astype(jnp.float32)).astype(jnp.bfloat16))
        high = jnp.concatenate(high, axis=0)
        low = jnp.concatenate(low, axis=0)
        out_ref[:, pair * LANES : (pair + 1) * LANES] = jnp.dot(
            restrict, high, preferred_element_type=jnp.float32
        ) + jnp.dot(restrict, low, preferred_element_type=jnp.float32)


def local(
    slabs,
    cols,
    fine_matrix,
    fine_columns,
    fine_counts,
    prolong,
    prolong_columns,
    restrict_rows,
    coarse_pattern,
):
    bricks = fine_counts.shape[0]
    owned = coarse_pattern.shape[1] // cols
    coarse = restrict_rows.shape[0] // BRICK * slabs
    packed = pack(prolong, prolong_columns)
    others = [swap(fine_matrix, "col", cols, d) for d in range(1, cols)]
    pieces, masks, others = gather_row(packed, slabs, others)
    fines = [pltpu.with_memory_space_constraint(fine_matrix, pltpu.VMEM)] + others
    rows = packed.shape[0]
    smem = pl.BlockSpec(memory_space=pltpu.SMEM)
    vmem = pl.BlockSpec(memory_space=pltpu.VMEM)
    held_rows = slabs * rows if len(pieces) > 1 else 16
    return pl.pallas_call(
        functools.partial(operator_kernel, slabs, masks, cols=cols),
        out_shape=jax.ShapeDtypeStruct((restrict_rows.shape[0], owned * BRICK), jnp.float32),
        in_specs=[smem] * 3 + [vmem] * (1 + cols + len(pieces)),
        out_specs=vmem,
        scratch_shapes=[
            pltpu.VMEM((held_rows, LANES), jnp.bfloat16),
            pltpu.VMEM((slabs, LANES), jnp.int32),
            pltpu.SMEM((slabs, LANES), jnp.int32),
            pltpu.SMEM((coarse + 1,), jnp.int32),
            pltpu.VMEM((bricks, owned + 1, BRICK, LANES), jnp.float32),
            pltpu.SemaphoreType.DMA,
        ],
        compiler_params=pltpu.CompilerParams(vmem_limit_bytes=32 * 1024 * 1024),
        name="operator",
    )(fine_columns, fine_counts, coarse_pattern, restrict_rows, *fines, *pieces)


def solution(mesh):
    return jax.shard_map(
        functools.partial(local, mesh.shape["row"], mesh.shape["col"]),
        mesh=mesh,
        in_specs=(
            P("row", "col"),
            P("row", None),
            P("row"),
            P("row", None),
            P("row", None),
            P("row", None),
            P("row", None),
        ),
        out_specs=P("row", "col"),
        check_vma=False,
    )
```

```python
import functools

import jax
import jax.numpy as jnp
from jax import lax
from jax.experimental import pallas as pl
from jax.experimental.pallas import tpu as pltpu
from jax.sharding import PartitionSpec as P

BRICK = 64
P_SLOTS = 2
DIGIT = 128
LANES = 128
EXTRA = 16


def pack_kernel(columns_ref, prolong_ref, packed_ref):
    rows = prolong_ref.shape[0]
    packed_ref[:rows, :] = prolong_ref[...]
    row = lax.broadcasted_iota(jnp.int32, (EXTRA, LANES), 0)
    lane = lax.broadcasted_iota(jnp.int32, (EXTRA, LANES), 1)
    digits = jnp.zeros((EXTRA, LANES), jnp.int32)
    for brick in range(columns_ref.shape[1]):
        for q in range(P_SLOTS):
            value = columns_ref[q, brick] + 1
            here = lane == brick
            digits = jnp.where(here & (row == 2 * q), lax.rem(value, DIGIT), digits)
            digits = jnp.where(here & (row == 2 * q + 1), lax.div(value, DIGIT), digits)
    packed_ref[rows:, :] = digits.astype(jnp.float32).astype(jnp.bfloat16)


def pack(prolong, prolong_columns):
    return pl.pallas_call(
        pack_kernel,
        out_shape=pltpu.VMEM((prolong.shape[0] + EXTRA, LANES), jnp.bfloat16),
        in_specs=[
            pl.BlockSpec(memory_space=pltpu.SMEM),
            pl.BlockSpec(memory_space=pltpu.VMEM),
        ],
        out_specs=pl.BlockSpec(memory_space=pltpu.VMEM),
        name="pack",
    )(prolong_columns.T, prolong)


def swap(block, axis, size, mask):
    return lax.ppermute(block, axis, [(i, i ^ mask) for i in range(size)])


def gather_row(packed, size, fine_other):
    if size != 16:
        return [lax.all_gather(packed, "row", axis=0, tiled=True)], None, fine_other
    got = {(0,): packed}
    for mask in (4, 8, 12):
        got[(mask,)] = swap(packed, "row", size, mask)
    across = {}
    for group in ((0, 4), (8,), (12,)):
        both = jnp.concatenate([got[(mask,)] for mask in group])
        across[tuple(mask | 2 for mask in group)] = swap(both, "row", size, 2)
    pieces = {**got, **across}
    for half in (got, across):
        both = jnp.concatenate(list(half.values()))
        if half is across:
            both, fine_other = lax.optimization_barrier((both, fine_other))
        group = tuple(mask | 1 for inside in half for mask in inside)
        pieces[group] = swap(both, "row", size, 1)
    return list(pieces.values()), list(pieces), fine_other


def index_kernel(by_xor, slabs, cols, columns_ref, counts_ref, pattern_ref, start_ref, pick_ref, own_ref):
    bricks, slots = columns_ref.shape
    share = slots // cols
    owned = pattern_ref.shape[1] // cols
    rows = bricks * BRICK + EXTRA
    row_index = lax.axis_index("row")
    col_index = lax.axis_index("col")
    lane = lax.broadcasted_iota(jnp.int32, (8, LANES), 1)
    slab_of = jnp.zeros((8, LANES), jnp.int32)
    inner_of = jnp.zeros((8, LANES), jnp.int32)
    live_of = jnp.zeros((8, LANES), jnp.int32)
    for i in range(bricks):
        for part in range(cols):
            first = (col_index ^ part) * share if cols > 1 else 0
            for pos in range(share):
                brick = columns_ref[i, first + pos]
                slab = lax.div(brick, bricks)
                inner = brick - slab * bricks
                if by_xor:
                    slab = slab ^ row_index
                here = lane == i * slots + part * share + pos
                slab_of = jnp.where(here, slab, slab_of)
                inner_of = jnp.where(here, inner, inner_of)
                live_of = jnp.where(here, (first + pos < counts_ref[i]).astype(jnp.int32), live_of)
    start_ref[...] = slab_of * rows + inner_of * BRICK
    place = jnp.where(live_of == 1, slab_of * bricks + inner_of, -1)[0:1, :]
    row = lax.broadcasted_iota(jnp.int32, pick_ref.shape, 0)
    pick_ref[...] = (row == place).astype(jnp.float32).astype(jnp.bfloat16)
    own = jnp.full(own_ref.shape, -1, jnp.int32)
    row = lax.broadcasted_iota(jnp.int32, own_ref.shape, 0)
    for s in range(owned):
        wanted = pattern_ref[0, col_index * owned + s]
        own = jnp.where(row == s, jnp.where(wanted < 0, -1, wanted + 1), own)
    own_ref[...] = own.astype(jnp.float32)


def make_index(by_xor, slabs, cols, fine_columns, fine_counts, coarse_pattern):
    bricks = fine_counts.shape[0]
    owned = coarse_pattern.shape[1] // cols
    up = lambda n, to: -(-n // to) * to
    return pl.pallas_call(
        functools.partial(index_kernel, by_xor, slabs, cols),
        out_shape=(
            pltpu.VMEM((8, LANES), jnp.int32),
            pltpu.VMEM((up(slabs * bricks, LANES), LANES), jnp.bfloat16),
            pltpu.VMEM((up(owned, 8), LANES), jnp.float32),
        ),
        in_specs=[pl.BlockSpec(memory_space=pltpu.SMEM)] * 3,
        out_specs=(pl.BlockSpec(memory_space=pltpu.VMEM),) * 3,
        name="index",
    )(fine_columns, fine_counts, coarse_pattern)


def operator_kernel(slabs, masks, bricks, slots, owned, start_ref, pick_ref, own_ref, restrict_ref, *refs, cols):
    parts = len(masks) if masks else 1
    fines, refs = refs[:cols], refs[cols:]
    pieces, refs = refs[:parts], refs[parts:]
    out_ref, held_ref, slot_ref, begin_ref, goal_ref, result_ref = refs[:6]
    sums, (begin_sem, goal_sem, out_sem) = refs[6 : 6 + bricks], refs[6 + bricks :]
    share = slots // cols
    rows = bricks * BRICK + EXTRA

    to_begin = pltpu.make_async_copy(start_ref, begin_ref, begin_sem)
    to_begin.start()
    table = [jnp.zeros((EXTRA, LANES), jnp.float32) for _ in range(pick_ref.shape[0] // LANES)]
    for piece, inside in zip(pieces, masks if masks else [range(slabs)]):
        for at, slab in enumerate(inside):
            first = at * rows + bricks * BRICK
            digits = piece[first : first + EXTRA, :].astype(jnp.float32)
            tile, shift = slab * bricks // LANES, slab * bricks % LANES
            table[tile] += pltpu.roll(digits, shift, 1) if shift else digits
    reached = jnp.dot(
        jnp.concatenate(table, axis=1).astype(jnp.bfloat16),
        pick_ref[...],
        preferred_element_type=jnp.float32,
    )
    own = own_ref[...]
    offset = lax.broadcasted_iota(jnp.int32, own.shape, 0).astype(jnp.float32) - owned
    for q in range(P_SLOTS):
        coarse = reached[2 * q : 2 * q + 1, :] + DIGIT * reached[2 * q + 1 : 2 * q + 2, :]
        slot = owned + jnp.sum(jnp.where(own == coarse, offset, 0.0), axis=0, keepdims=True)
        slot_ref[q : q + 1, :] = slot.astype(jnp.int32)
    to_goal = pltpu.make_async_copy(slot_ref, goal_ref, goal_sem)
    to_goal.start()

    source = pieces[0]
    if masks:
        source = held_ref
        for piece, inside in zip(pieces, masks):
            for at, slab in enumerate(inside):
                held_ref[slab * rows : (slab + 1) * rows, :] = piece[at * rows : (at + 1) * rows, :]
    for total in sums:
        total[...] = jnp.zeros_like(total)
    left = lax.broadcasted_iota(jnp.int32, (BRICK, LANES), 1) < BRICK
    nothing = jnp.zeros((BRICK, LANES), jnp.bfloat16)

    to_begin.wait()
    to_goal.wait()

    for part in range(cols):
        for pair in range(share // 2):
            for i in range(bricks):
                blocks, where_to = [], []
                for half in range(2):
                    at = i * slots + part * share + pair * 2 + half
                    start = pl.multiple_of(begin_ref[0, at], 16)
                    blocks.append(source[pl.ds(start, BRICK), :])
                    where_to += [goal_ref[q, at] for q in range(P_SLOTS)]
                right = jnp.concatenate(
                    [
                        jnp.concatenate([blocks[0], nothing], axis=1),
                        jnp.concatenate([nothing, blocks[1]], axis=1),
                    ],
                    axis=0,
                )
                a = fines[part][i * BRICK : (i + 1) * BRICK, pair * LANES : (pair + 1) * LANES]
                product = jnp.dot(a, right, preferred_element_type=jnp.float32)
                for half in range(2):
                    block = product[:, half * LANES : (half + 1) * LANES]
                    sums[i][where_to[half * 2]] += jnp.where(left, block, 0.0)
                    sums[i][where_to[half * 2 + 1]] += jnp.where(left, 0.0, block)

    restrict = restrict_ref[...]
    group = 4 if owned % 4 == 0 else 2
    width = group * BRICK
    leaving = []
    for at in range(owned // group):
        high, low = [], []
        for i in range(bricks):
            tops, rests = [], []
            for even in range(at * group, (at + 1) * group, 2):
                first, second = sums[i][even], sums[i][even + 1]
                total = jnp.where(left, first, second) + pltpu.roll(
                    jnp.where(left, second, first), BRICK, 1
                )
                tops.append(total.astype(jnp.bfloat16))
                rests.append((total - tops[-1].astype(jnp.float32)).astype(jnp.bfloat16))
            high.append(jnp.concatenate(tops, axis=1))
            low.append(jnp.concatenate(rests, axis=1))
        high = jnp.concatenate(high, axis=0)
        low = jnp.concatenate(low, axis=0)
        here = pl.ds(at * width, width)
        result_ref[:, here] = jnp.dot(restrict, high, preferred_element_type=jnp.float32) + jnp.dot(
            restrict, low, preferred_element_type=jnp.float32
        )
        move = pltpu.make_async_copy(result_ref.at[:, here], out_ref.at[:, here], out_sem.at[at])
        move.start()
        leaving.append(move)
    for move in leaving:
        move.wait()


def operate(slabs, cols, bricks, slots, owned, index, restrict_rows, fines, pieces, masks):
    rows = bricks * BRICK + EXTRA
    vmem = pl.BlockSpec(memory_space=pltpu.VMEM)
    held_rows = slabs * rows if masks else 16
    shape = (restrict_rows.shape[0], owned * BRICK)
    return pl.pallas_call(
        functools.partial(operator_kernel, slabs, masks, bricks, slots, owned, cols=cols),
        out_shape=jax.ShapeDtypeStruct(shape, jnp.float32),
        in_specs=[vmem] * (4 + cols + len(pieces)),
        out_specs=pl.BlockSpec(memory_space=pl.ANY),
        scratch_shapes=[
            pltpu.VMEM((held_rows, LANES), jnp.bfloat16),
            pltpu.VMEM((8, LANES), jnp.int32),
            pltpu.SMEM((8, LANES), jnp.int32),
            pltpu.SMEM((8, LANES), jnp.int32),
            pltpu.VMEM(shape, jnp.float32),
        ]
        + [pltpu.VMEM((owned + 1, BRICK, LANES), jnp.float32)] * bricks
        + [
            pltpu.SemaphoreType.DMA,
            pltpu.SemaphoreType.DMA,
            pltpu.SemaphoreType.DMA((owned // 2,)),
        ],
        compiler_params=pltpu.CompilerParams(vmem_limit_bytes=32 * 1024 * 1024),
        name="operator",
    )(*index, restrict_rows, *fines, *pieces)


def local(
    slabs,
    cols,
    fine_matrix,
    fine_columns,
    fine_counts,
    prolong,
    prolong_columns,
    restrict_rows,
    coarse_pattern,
):
    bricks, slots = fine_columns.shape
    owned = coarse_pattern.shape[1] // cols
    packed = pack(prolong, prolong_columns)
    others = [swap(fine_matrix, "col", cols, d) for d in range(1, cols)]
    pieces, masks, others = gather_row(packed, slabs, others)
    fines = [pltpu.with_memory_space_constraint(fine_matrix, pltpu.VMEM)] + others
    if masks:
        fine_columns, pieces[1] = lax.optimization_barrier((fine_columns, pieces[1]))
    index = make_index(masks is not None, slabs, cols, fine_columns, fine_counts, coarse_pattern)
    return operate(slabs, cols, bricks, slots, owned, index, restrict_rows, fines, pieces, masks)


def solution(mesh):
    return jax.shard_map(
        functools.partial(local, mesh.shape["row"], mesh.shape["col"]),
        mesh=mesh,
        in_specs=(
            P("row", "col"),
            P("row", None),
            P("row"),
            P("row", None),
            P("row", None),
            P("row", None),
            P("row", None),
        ),
        out_specs=P("row", "col"),
        check_vma=False,
    )
```

```python
import functools

import jax
import jax.numpy as jnp
from jax import lax
from jax.experimental import pallas as pl
from jax.experimental.pallas import tpu as pltpu
from jax.sharding import PartitionSpec as P

BRICK = 64
P_SLOTS = 2
DIGIT = 128
LANES = 128
EXTRA = 16
SMALL = 8 * 1024 * 1024


def pack_kernel(columns_ref, prolong_ref, packed_ref):
    rows = prolong_ref.shape[0]
    packed_ref[:rows, :] = prolong_ref[...]
    row = lax.broadcasted_iota(jnp.int32, (EXTRA, LANES), 0)
    lane = lax.broadcasted_iota(jnp.int32, (EXTRA, LANES), 1)
    digits = jnp.zeros((EXTRA, LANES), jnp.int32)
    for brick in range(columns_ref.shape[1]):
        for q in range(P_SLOTS):
            value = columns_ref[q, brick] + 1
            here = lane == brick
            digits = jnp.where(here & (row == 2 * q), lax.rem(value, DIGIT), digits)
            digits = jnp.where(here & (row == 2 * q + 1), lax.div(value, DIGIT), digits)
    packed_ref[rows:, :] = digits.astype(jnp.float32).astype(jnp.bfloat16)


def pack(prolong, prolong_columns):
    return pl.pallas_call(
        pack_kernel,
        out_shape=pltpu.VMEM((prolong.shape[0] + EXTRA, LANES), jnp.bfloat16),
        in_specs=[
            pl.BlockSpec(memory_space=pltpu.SMEM),
            pl.BlockSpec(memory_space=pltpu.VMEM),
        ],
        out_specs=pl.BlockSpec(memory_space=pltpu.VMEM),
        name="pack",
    )(prolong_columns.T, prolong)


def swap(block, axis, size, mask):
    return lax.ppermute(block, axis, [(i, i ^ mask) for i in range(size)])


def gather_row(packed, size, fine_other, make):
    if size != 16:
        return [lax.all_gather(packed, "row", axis=0, tiled=True)], None, fine_other, make(packed)
    got = {(0,): packed}
    for mask in (4, 8, 12):
        got[(mask,)] = swap(packed, "row", size, mask)
    across = {}
    for group in ((0, 4), (8,), (12,)):
        both = jnp.concatenate([got[(mask,)] for mask in group])
        across[tuple(mask | 2 for mask in group)] = swap(both, "row", size, 2)
    index = list(make(got[(4,)]))
    pieces = {**got, **across}
    for half in (got, across):
        both = jnp.concatenate(list(half.values()))
        if half is across:
            both, fine_other, index[1] = lax.optimization_barrier((both, fine_other, index[1]))
        group = tuple(mask | 1 for inside in half for mask in inside)
        pieces[group] = swap(both, "row", size, 1)
    return list(pieces.values()), list(pieces), fine_other, index


def index_kernel(by_xor, slabs, cols, columns_ref, counts_ref, pattern_ref, start_ref, pick_ref, own_ref, *sums):
    bricks, slots = columns_ref.shape
    share = slots // cols
    owned = pattern_ref.shape[1] // cols
    rows = bricks * BRICK + EXTRA
    row_index = lax.axis_index("row")
    col_index = lax.axis_index("col")
    lane = lax.broadcasted_iota(jnp.int32, (8, LANES), 1)
    slab_of = jnp.zeros((8, LANES), jnp.int32)
    inner_of = jnp.zeros((8, LANES), jnp.int32)
    live_of = jnp.zeros((8, LANES), jnp.int32)
    for i in range(bricks):
        for part in range(cols):
            first = (col_index ^ part) * share if cols > 1 else 0
            for pos in range(share):
                brick = columns_ref[i, first + pos]
                slab = lax.div(brick, bricks)
                inner = brick - slab * bricks
                if by_xor:
                    slab = slab ^ row_index
                start_ref[0, i * slots + part * share + pos] = slab * rows + inner * BRICK
                here = lane == i * slots + part * share + pos
                slab_of = jnp.where(here, slab, slab_of)
                inner_of = jnp.where(here, inner, inner_of)
                live_of = jnp.where(here, (first + pos < counts_ref[i]).astype(jnp.int32), live_of)
    place = jnp.where(live_of == 1, slab_of * bricks + inner_of, -1)[0:1, :]
    row = lax.broadcasted_iota(jnp.int32, pick_ref.shape, 0)
    pick_ref[...] = (row == place).astype(jnp.float32).astype(jnp.bfloat16)
    own = jnp.full(own_ref.shape, -1, jnp.int32)
    row = lax.broadcasted_iota(jnp.int32, own_ref.shape, 0)
    for s in range(owned):
        wanted = pattern_ref[0, col_index * owned + s]
        own = jnp.where(row == s, jnp.where(wanted < 0, -1, wanted + 1), own)
    own_ref[...] = own.astype(jnp.float32)
    for total in sums:
        total[...] = jnp.zeros_like(total)


def make_index(by_xor, slabs, cols, fine_columns, fine_counts, coarse_pattern):
    bricks = fine_counts.shape[0]
    owned = coarse_pattern.shape[1] // cols
    slots = fine_columns.shape[1]
    up = lambda n, to: -(-n // to) * to
    return pl.pallas_call(
        functools.partial(index_kernel, by_xor, slabs, cols),
        out_shape=(
            pltpu.SMEM((1, bricks * slots), jnp.int32),
            pltpu.VMEM((up(slabs * bricks, LANES), LANES), jnp.bfloat16),
            pltpu.VMEM((up(owned, 8), LANES), jnp.float32),
        )
        + (pltpu.VMEM((owned + 1, BRICK, LANES), jnp.float32),) * (bricks * P_SLOTS),
        in_specs=[pl.BlockSpec(memory_space=pltpu.SMEM)] * 3,
        out_specs=(pl.BlockSpec(memory_space=pltpu.SMEM),) + (pl.BlockSpec(memory_space=pltpu.VMEM),) * (2 + bricks * P_SLOTS),
        compiler_params=pltpu.CompilerParams(vmem_limit_bytes=SMALL),
        name="index",
    )(fine_columns, fine_counts, coarse_pattern)


def operator_kernel(slabs, masks, bricks, slots, owned, start_ref, pick_ref, own_ref, restrict_ref, *refs, cols):
    parts = len(masks) if masks else 1
    fines, refs = refs[:cols], refs[cols:]
    pieces, refs = refs[:parts], refs[parts:]
    refs = refs[bricks * P_SLOTS :]
    out_ref, refs = refs[0], refs[1:]
    sums, refs = refs[: bricks * P_SLOTS], refs[bricks * P_SLOTS :]
    held_ref, result_ref, out_sem = refs
    share = slots // cols
    rows = bricks * BRICK + EXTRA

    table = [jnp.zeros((EXTRA, LANES), jnp.float32) for _ in range(pick_ref.shape[0] // LANES)]
    for piece, inside in zip(pieces, masks if masks else [range(slabs)]):
        for at, slab in enumerate(inside):
            first = at * rows + bricks * BRICK
            digits = piece[first : first + EXTRA, :].astype(jnp.float32)
            tile, shift = slab * bricks // LANES, slab * bricks % LANES
            table[tile] += pltpu.roll(digits, shift, 1) if shift else digits
    reached = jnp.dot(
        jnp.concatenate(table, axis=1).astype(jnp.bfloat16),
        pick_ref[...],
        preferred_element_type=jnp.float32,
    )
    own = own_ref[...]
    slots_v = []
    offset = lax.broadcasted_iota(jnp.int32, own.shape, 0).astype(jnp.float32) - owned
    for q in range(P_SLOTS):
        coarse = reached[2 * q : 2 * q + 1, :] + DIGIT * reached[2 * q + 1 : 2 * q + 2, :]
        slot = owned + jnp.sum(jnp.where(own == coarse, offset, 0.0), axis=0, keepdims=True)
        slots_v.append(slot.astype(jnp.int32))

    source = pieces[0]
    if masks:
        source = held_ref
        for piece, inside in zip(pieces, masks):
            for at, slab in enumerate(inside):
                held_ref[slab * rows : (slab + 1) * rows, :] = piece[at * rows : (at + 1) * rows, :]
    left = lax.broadcasted_iota(jnp.int32, (BRICK, LANES), 1) < BRICK
    nothing = jnp.zeros((BRICK, LANES), jnp.bfloat16)


    for part in range(cols):
        for pair in range(share // 2):
            for i in range(bricks):
                blocks, where_to = [], []
                for half in range(2):
                    at = i * slots + part * share + pair * 2 + half
                    start = pl.multiple_of(start_ref[0, at], 16)
                    blocks.append(source[pl.ds(start, BRICK), :])
                    where_to += [slots_v[q][0, at] for q in range(P_SLOTS)]
                right = jnp.concatenate(
                    [
                        jnp.concatenate([blocks[0], nothing], axis=1),
                        jnp.concatenate([nothing, blocks[1]], axis=1),
                    ],
                    axis=0,
                )
                a = fines[part][i * BRICK : (i + 1) * BRICK, pair * LANES : (pair + 1) * LANES]
                product = jnp.dot(a, right, preferred_element_type=jnp.float32)
                for half in range(2):
                    block = product[:, half * LANES : (half + 1) * LANES]
                    sums[i*2+0+2*0][where_to[half * 2]] += block
                    sums[i*2+1+2*0][where_to[half * 2 + 1]] += block

    restrict = restrict_ref[...]
    group = 4 if owned % 4 == 0 else 2
    width = group * BRICK
    leaving = []
    for at in range(owned // group):
        high, low = [], []
        for i in range(bricks):
            tops, rests = [], []
            for even in range(at * group, (at + 1) * group, 2):
                f0, f1, s0, s1 = sums[2*i][even], sums[2*i+1][even], sums[2*i][even + 1], sums[2*i+1][even+1]
                total = jnp.where(left, f0, s1) + pltpu.roll(
                    jnp.where(left, s0, f1), BRICK, 1
                )
                tops.append(total.astype(jnp.bfloat16))
                rests.append((total - tops[-1].astype(jnp.float32)).astype(jnp.bfloat16))
            high.append(jnp.concatenate(tops, axis=1))
            low.append(jnp.concatenate(rests, axis=1))
        high = jnp.concatenate(high, axis=0)
        low = jnp.concatenate(low, axis=0)
        here = pl.ds(at * width, width)
        result_ref[:, here] = jnp.dot(restrict, high, preferred_element_type=jnp.float32) + jnp.dot(
            restrict, low, preferred_element_type=jnp.float32
        )
        move = pltpu.make_async_copy(result_ref.at[:, here], out_ref.at[:, here], out_sem.at[at])
        move.start()
        leaving.append(move)
    for move in leaving:
        move.wait()


def operate(slabs, cols, bricks, slots, owned, index, restrict_rows, fines, pieces, masks):
    rows = bricks * BRICK + EXTRA
    vmem = pl.BlockSpec(memory_space=pltpu.VMEM)
    smem = pl.BlockSpec(memory_space=pltpu.SMEM)
    held_rows = slabs * rows if masks else 16
    shape = (restrict_rows.shape[0], owned * BRICK)
    starts, pick, own, *sums = index
    starts = pltpu.with_memory_space_constraint(starts, pltpu.SMEM)
    given = (starts, pick, own, restrict_rows, *fines, *pieces)
    return pl.pallas_call(
        functools.partial(operator_kernel, slabs, masks, bricks, slots, owned, cols=cols),
        out_shape=[jax.ShapeDtypeStruct(shape, jnp.float32)]
        + [pltpu.VMEM(each.shape, jnp.float32) for each in sums],
        in_specs=[smem] + [vmem] * (len(given) - 1 + len(sums)),
        out_specs=[pl.BlockSpec(memory_space=pl.ANY)] + [vmem] * len(sums),
        input_output_aliases={len(given) + at: 1 + at for at in range(len(sums))},
        scratch_shapes=[
            pltpu.VMEM((held_rows, LANES), jnp.bfloat16),
            pltpu.VMEM(shape, jnp.float32),
            pltpu.SemaphoreType.DMA((owned // 2,)),
        ],
        compiler_params=pltpu.CompilerParams(vmem_limit_bytes=32 * 1024 * 1024),
        name="operator",
    )(*given, *sums)[0]


def local(
    slabs,
    cols,
    fine_matrix,
    fine_columns,
    fine_counts,
    prolong,
    prolong_columns,
    restrict_rows,
    coarse_pattern,
):
    bricks, slots = fine_columns.shape
    owned = coarse_pattern.shape[1] // cols
    packed = pack(prolong, prolong_columns)
    others = [swap(fine_matrix, "col", cols, d) for d in range(1, cols)]

    def make(after):
        columns, _ = lax.optimization_barrier((fine_columns, after))
        return make_index(slabs == 16, slabs, cols, columns, fine_counts, coarse_pattern)

    pieces, masks, others, index = gather_row(packed, slabs, others, make)
    fines = [pltpu.with_memory_space_constraint(fine_matrix, pltpu.VMEM)] + others
    return operate(slabs, cols, bricks, slots, owned, index, restrict_rows, fines, pieces, masks)


def solution(mesh):
    return jax.shard_map(
        functools.partial(local, mesh.shape["row"], mesh.shape["col"]),
        mesh=mesh,
        in_specs=(
            P("row", "col"),
            P("row", None),
            P("row"),
            P("row", None),
            P("row", None),
            P("row", None),
            P("row", None),
        ),
        out_specs=P("row", "col"),
        check_vma=False,
    )
```

```python
import functools

import jax
import jax.numpy as jnp
from jax import lax
from jax.experimental import pallas as pl
from jax.experimental.pallas import tpu as pltpu
from jax.sharding import PartitionSpec as P

BRICK = 64
P_SLOTS = 2
DIGIT = 128
LANES = 128
EXTRA = 16
SMALL = 8 * 1024 * 1024


def pack_kernel(columns_ref, prolong_ref, packed_ref):
    rows = prolong_ref.shape[0]
    packed_ref[:rows, :] = prolong_ref[...]
    row = lax.broadcasted_iota(jnp.int32, (EXTRA, LANES), 0)
    lane = lax.broadcasted_iota(jnp.int32, (EXTRA, LANES), 1)
    digits = jnp.zeros((EXTRA, LANES), jnp.int32)
    for brick in range(columns_ref.shape[1]):
        for q in range(P_SLOTS):
            value = columns_ref[q, brick] + 1
            here = lane == brick
            digits = jnp.where(here & (row == 2 * q), lax.rem(value, DIGIT), digits)
            digits = jnp.where(here & (row == 2 * q + 1), lax.div(value, DIGIT), digits)
    packed_ref[rows:, :] = digits.astype(jnp.float32).astype(jnp.bfloat16)


def pack(prolong, prolong_columns):
    return pl.pallas_call(
        pack_kernel,
        out_shape=pltpu.VMEM((prolong.shape[0] + EXTRA, LANES), jnp.bfloat16),
        in_specs=[
            pl.BlockSpec(memory_space=pltpu.SMEM),
            pl.BlockSpec(memory_space=pltpu.VMEM),
        ],
        out_specs=pl.BlockSpec(memory_space=pltpu.VMEM),
        name="pack",
    )(prolong_columns.T, prolong)


def swap(block, axis, size, mask):
    return lax.ppermute(block, axis, [(i, i ^ mask) for i in range(size)])


def gather_row(packed, size, make):
    if size != 16:
        return [lax.all_gather(packed, "row", axis=0, tiled=True)], None, make(packed)
    got = {(0,): packed}
    for mask in (4, 12, 8):
        got[(mask,)] = swap(packed, "row", size, mask)
    across = {}
    for group in ((12,), (0,), (4,), (8,)):
        both = jnp.concatenate([got[(mask,)] for mask in group])
        across[tuple(mask | 2 for mask in group)] = swap(both, "row", size, 2)
    index = list(make(got[(8,)]))
    pieces = {**got, **across}
    for half in (((12,), (4,), (8,), (0,)), ((6,), (14,), (2,), (10,))):
        both = jnp.concatenate([pieces[inside] for inside in half])
        if half[0] in across:
            both, index[1] = lax.optimization_barrier((both, index[1]))
        group = tuple(mask | 1 for inside in half for mask in inside)
        pieces[group] = swap(both, "row", size, 1)
    return list(pieces.values()), list(pieces), index


def index_kernel(by_xor, slabs, cols, columns_ref, counts_ref, pattern_ref, start_ref, pick_ref, own_ref, *sums):
    bricks, slots = columns_ref.shape
    share = slots // cols
    owned = pattern_ref.shape[1] // cols
    rows = bricks * BRICK + EXTRA
    row_index = lax.axis_index("row")
    col_index = lax.axis_index("col")
    lane = lax.broadcasted_iota(jnp.int32, (8, LANES), 1)
    slab_of = jnp.zeros((8, LANES), jnp.int32)
    inner_of = jnp.zeros((8, LANES), jnp.int32)
    live_of = jnp.zeros((8, LANES), jnp.int32)
    for i in range(bricks):
        for part in range(cols):
            first = (col_index ^ part) * share if cols > 1 else 0
            for pos in range(share):
                brick = columns_ref[i, first + pos]
                slab = lax.div(brick, bricks)
                inner = brick - slab * bricks
                if by_xor:
                    slab = slab ^ row_index
                start_ref[0, i * slots + part * share + pos] = slab * rows + inner * BRICK
                here = lane == i * slots + part * share + pos
                slab_of = jnp.where(here, slab, slab_of)
                inner_of = jnp.where(here, inner, inner_of)
                live_of = jnp.where(here, (first + pos < counts_ref[i]).astype(jnp.int32), live_of)
    place = jnp.where(live_of == 1, slab_of * bricks + inner_of, -1)[0:1, :]
    row = lax.broadcasted_iota(jnp.int32, pick_ref.shape, 0)
    pick_ref[...] = (row == place).astype(jnp.float32).astype(jnp.bfloat16)
    own = jnp.full(own_ref.shape, -1, jnp.int32)
    row = lax.broadcasted_iota(jnp.int32, own_ref.shape, 0)
    for s in range(owned):
        wanted = pattern_ref[0, col_index * owned + s]
        own = jnp.where(row == s, jnp.where(wanted < 0, -1, wanted + 1), own)
    own_ref[...] = own.astype(jnp.float32)
    for total in sums:
        total[...] = jnp.zeros_like(total)


def make_index(by_xor, slabs, cols, fine_columns, fine_counts, coarse_pattern):
    bricks = fine_counts.shape[0]
    owned = coarse_pattern.shape[1] // cols
    slots = fine_columns.shape[1]
    up = lambda n, to: -(-n // to) * to
    return pl.pallas_call(
        functools.partial(index_kernel, by_xor, slabs, cols),
        out_shape=(
            pltpu.SMEM((1, bricks * slots), jnp.int32),
            pltpu.VMEM((up(slabs * bricks, LANES), LANES), jnp.bfloat16),
            pltpu.VMEM((up(owned, 8), LANES), jnp.float32),
        )
        + (pltpu.VMEM((owned + 1, BRICK, LANES), jnp.float32),) * (bricks * P_SLOTS),
        in_specs=[pl.BlockSpec(memory_space=pltpu.SMEM)] * 3,
        out_specs=(pl.BlockSpec(memory_space=pltpu.SMEM),) + (pl.BlockSpec(memory_space=pltpu.VMEM),) * (2 + bricks * P_SLOTS),
        compiler_params=pltpu.CompilerParams(vmem_limit_bytes=SMALL),
        name="index",
    )(fine_columns, fine_counts, coarse_pattern)


def operator_kernel(slabs, masks, bricks, slots, owned, start_ref, pick_ref, own_ref, restrict_ref, *refs, cols):
    parts = len(masks) if masks else 1
    fines, refs = refs[:cols], refs[cols:]
    pieces, refs = refs[:parts], refs[parts:]
    refs = refs[bricks * P_SLOTS :]
    out_ref, refs = refs[0], refs[1:]
    sums, refs = refs[: bricks * P_SLOTS], refs[bricks * P_SLOTS :]
    held_ref, result_ref, out_sem = refs
    share = slots // cols
    rows = bricks * BRICK + EXTRA

    table = [jnp.zeros((EXTRA, LANES), jnp.float32) for _ in range(pick_ref.shape[0] // LANES)]
    for piece, inside in zip(pieces, masks if masks else [range(slabs)]):
        for at, slab in enumerate(inside):
            first = at * rows + bricks * BRICK
            digits = piece[first : first + EXTRA, :].astype(jnp.float32)
            tile, shift = slab * bricks // LANES, slab * bricks % LANES
            table[tile] += pltpu.roll(digits, shift, 1) if shift else digits
    reached = jnp.dot(
        jnp.concatenate(table, axis=1).astype(jnp.bfloat16),
        pick_ref[...],
        preferred_element_type=jnp.float32,
    )
    own = own_ref[...]
    slots_v = []
    offset = lax.broadcasted_iota(jnp.int32, own.shape, 0).astype(jnp.float32) - owned
    for q in range(P_SLOTS):
        coarse = reached[2 * q : 2 * q + 1, :] + DIGIT * reached[2 * q + 1 : 2 * q + 2, :]
        slot = owned + jnp.sum(jnp.where(own == coarse, offset, 0.0), axis=0, keepdims=True)
        slots_v.append(slot.astype(jnp.int32))
    goals = slots_v[0] + 256 * slots_v[1]

    source = pieces[0]
    if masks:
        source = held_ref
        for piece, inside in zip(pieces, masks):
            for at, slab in enumerate(inside):
                held_ref[slab * rows : (slab + 1) * rows, :] = piece[at * rows : (at + 1) * rows, :]
    left = lax.broadcasted_iota(jnp.int32, (BRICK, LANES), 1) < BRICK
    nothing = jnp.zeros((BRICK, LANES), jnp.bfloat16)


    for part in range(cols):
        for pair in range(share // 2):
            for i in range(bricks):
                blocks, where_to = [], []
                for half in range(2):
                    at = i * slots + part * share + pair * 2 + half
                    start = pl.multiple_of(start_ref[0, at], 16)
                    blocks.append(source[pl.ds(start, BRICK), :])
                    goal = goals[0, at]
                    where_to += [goal & 255, goal >> 8]
                right = jnp.concatenate(
                    [
                        jnp.concatenate([blocks[0], nothing], axis=1),
                        jnp.concatenate([nothing, blocks[1]], axis=1),
                    ],
                    axis=0,
                )
                a = fines[part][i * BRICK : (i + 1) * BRICK, pair * LANES : (pair + 1) * LANES]
                product = jnp.dot(a, right, preferred_element_type=jnp.float32)
                for half in range(2):
                    block = product[:, half * LANES : (half + 1) * LANES]
                    sums[i*2+0+2*0][where_to[half * 2]] += block
                    sums[i*2+1+2*0][where_to[half * 2 + 1]] += block

    restrict = restrict_ref[...]
    group = 2
    width = group * BRICK
    leaving = []
    for at in range(owned // group):
        high, low = [], []
        for i in range(bricks):
            tops, rests = [], []
            for even in range(at * group, (at + 1) * group, 2):
                f0, f1, s0, s1 = sums[2*i][even], sums[2*i+1][even], sums[2*i][even + 1], sums[2*i+1][even+1]
                total = jnp.where(left, f0, s1) + pltpu.roll(
                    jnp.where(left, s0, f1), BRICK, 1
                )
                tops.append(total.astype(jnp.bfloat16))
                rests.append((total - tops[-1].astype(jnp.float32)).astype(jnp.bfloat16))
            high.append(jnp.concatenate(tops, axis=1))
            low.append(jnp.concatenate(rests, axis=1))
        high = jnp.concatenate(high, axis=0)
        low = jnp.concatenate(low, axis=0)
        here = pl.ds(at * width, width)
        result_ref[:, here] = jnp.dot(restrict, high, preferred_element_type=jnp.float32) + jnp.dot(
            restrict, low, preferred_element_type=jnp.float32
        )
        move = pltpu.make_async_copy(result_ref.at[:, here], out_ref.at[:, here], out_sem.at[at])
        move.start()
        leaving.append(move)
    for move in leaving:
        move.wait()


def operate(slabs, cols, bricks, slots, owned, index, restrict_rows, fines, pieces, masks):
    rows = bricks * BRICK + EXTRA
    vmem = pl.BlockSpec(memory_space=pltpu.VMEM)
    smem = pl.BlockSpec(memory_space=pltpu.SMEM)
    held_rows = slabs * rows if masks else 16
    shape = (restrict_rows.shape[0], owned * BRICK)
    starts, pick, own, *sums = index
    starts = pltpu.with_memory_space_constraint(starts, pltpu.SMEM)
    given = (starts, pick, own, restrict_rows, *fines, *pieces)
    return pl.pallas_call(
        functools.partial(operator_kernel, slabs, masks, bricks, slots, owned, cols=cols),
        out_shape=[jax.ShapeDtypeStruct(shape, jnp.float32)]
        + [pltpu.VMEM(each.shape, jnp.float32) for each in sums],
        in_specs=[smem] + [vmem] * (len(given) - 1 + len(sums)),
        out_specs=[pl.BlockSpec(memory_space=pl.ANY)] + [vmem] * len(sums),
        input_output_aliases={len(given) + at: 1 + at for at in range(len(sums))},
        scratch_shapes=[
            pltpu.VMEM((held_rows, LANES), jnp.bfloat16),
            pltpu.VMEM(shape, jnp.float32),
            pltpu.SemaphoreType.DMA((owned // 2,)),
        ],
        compiler_params=pltpu.CompilerParams(vmem_limit_bytes=32 * 1024 * 1024),
        name="operator",
    )(*given, *sums)[0]


def local(
    slabs,
    cols,
    fine_matrix,
    fine_columns,
    fine_counts,
    prolong,
    prolong_columns,
    restrict_rows,
    coarse_pattern,
):
    bricks, slots = fine_columns.shape
    owned = coarse_pattern.shape[1] // cols
    packed = pack(prolong, prolong_columns)
    others = [swap(fine_matrix, "col", cols, d) for d in range(1, cols)]

    def make(after):
        columns, _ = lax.optimization_barrier((fine_columns, after))
        return make_index(slabs == 16, slabs, cols, columns, fine_counts, coarse_pattern)

    pieces, masks, index = gather_row(packed, slabs, make)
    fines = [pltpu.with_memory_space_constraint(fine_matrix, pltpu.VMEM)] + others
    return operate(slabs, cols, bricks, slots, owned, index, restrict_rows, fines, pieces, masks)


def solution(mesh):
    return jax.shard_map(
        functools.partial(local, mesh.shape["row"], mesh.shape["col"]),
        mesh=mesh,
        in_specs=(
            P("row", "col"),
            P("row", None),
            P("row"),
            P("row", None),
            P("row", None),
            P("row", None),
            P("row", None),
        ),
        out_specs=P("row", "col"),
        check_vma=False,
    )
```

```python
import functools

import jax
import jax.numpy as jnp
from jax import lax
from jax.experimental import pallas as pl
from jax.experimental.pallas import tpu as pltpu
from jax.sharding import PartitionSpec as P

BRICK = 64
P_SLOTS = 2
DIGIT = 128
LANES = 128
EXTRA = 16
GOAL_BITS = 8
GOAL = 1 << GOAL_BITS
SMALL = 8 * 1024 * 1024


def pack_kernel(columns_ref, prolong_ref, packed_ref):
    rows = prolong_ref.shape[0]
    packed_ref[:rows, :] = prolong_ref[...]
    row = lax.broadcasted_iota(jnp.int32, (EXTRA, LANES), 0)
    lane = lax.broadcasted_iota(jnp.int32, (EXTRA, LANES), 1)
    digits = jnp.zeros((EXTRA, LANES), jnp.int32)
    for brick in range(columns_ref.shape[1]):
        for q in range(P_SLOTS):
            value = columns_ref[q, brick] + 1
            here = lane == brick
            digits = jnp.where(here & (row == 2 * q), lax.rem(value, DIGIT), digits)
            digits = jnp.where(here & (row == 2 * q + 1), lax.div(value, DIGIT), digits)
    packed_ref[rows:, :] = digits.astype(jnp.float32).astype(jnp.bfloat16)


def pack(prolong, prolong_columns):
    return pl.pallas_call(
        pack_kernel,
        out_shape=pltpu.VMEM((prolong.shape[0] + EXTRA, LANES), jnp.bfloat16),
        in_specs=[
            pl.BlockSpec(memory_space=pltpu.SMEM),
            pl.BlockSpec(memory_space=pltpu.VMEM),
        ],
        out_specs=pl.BlockSpec(memory_space=pltpu.VMEM),
        name="pack",
    )(prolong_columns.T, prolong)


def swap(block, axis, size, mask):
    return lax.ppermute(block, axis, [(i, i ^ mask) for i in range(size)])


def gather_row(packed, size, make):
    if size != 16:
        return [lax.all_gather(packed, "row", axis=0, tiled=True)], None, make(packed)
    got = {(0,): packed}
    for mask in (8, 12, 4):
        got[(mask,)] = swap(packed, "row", size, mask)
    across = {}
    for group in ((12,), (0,), (4,), (8,)):
        both = jnp.concatenate([got[(mask,)] for mask in group])
        across[tuple(mask | 2 for mask in group)] = swap(both, "row", size, 2)
    index = list(make(got[(8,)]))
    pieces = {**got, **across}
    for half in (((0,), (8,), (4,), (12,)), ((6,), (14,), (2,), (10,))):
        both = jnp.concatenate([pieces[inside] for inside in half])
        if half[0] in across:
            both, index[1] = lax.optimization_barrier((both, index[1]))
        group = tuple(mask | 1 for inside in half for mask in inside)
        pieces[group] = swap(both, "row", size, 1)
    return list(pieces.values()), list(pieces), index


def index_kernel(
    by_xor, slabs, cols, columns_ref, counts_ref, pattern_ref, start_ref, pick_ref, own_ref, *sums
):
    bricks, slots = columns_ref.shape
    share = slots // cols
    owned = pattern_ref.shape[1] // cols
    rows = bricks * BRICK + EXTRA
    row_index = lax.axis_index("row")
    col_index = lax.axis_index("col")
    lane = lax.broadcasted_iota(jnp.int32, (8, LANES), 1)
    slab_of = jnp.zeros((8, LANES), jnp.int32)
    inner_of = jnp.zeros((8, LANES), jnp.int32)
    live_of = jnp.zeros((8, LANES), jnp.int32)
    for i in range(bricks):
        for part in range(cols):
            first = (col_index ^ part) * share if cols > 1 else 0
            for pos in range(share):
                brick = columns_ref[i, first + pos]
                slab = lax.div(brick, bricks)
                inner = brick - slab * bricks
                if by_xor:
                    slab = slab ^ row_index
                start_ref[0, i * slots + part * share + pos] = slab * rows + inner * BRICK
                here = lane == i * slots + part * share + pos
                slab_of = jnp.where(here, slab, slab_of)
                inner_of = jnp.where(here, inner, inner_of)
                live_of = jnp.where(here, (first + pos < counts_ref[i]).astype(jnp.int32), live_of)
    place = jnp.where(live_of == 1, slab_of * bricks + inner_of, -1)[0:1, :]
    row = lax.broadcasted_iota(jnp.int32, pick_ref.shape, 0)
    pick_ref[...] = (row == place).astype(jnp.float32).astype(jnp.bfloat16)
    own = jnp.full(own_ref.shape, -1, jnp.int32)
    row = lax.broadcasted_iota(jnp.int32, own_ref.shape, 0)
    for s in range(owned):
        wanted = pattern_ref[0, col_index * owned + s]
        own = jnp.where(row == s, jnp.where(wanted < 0, -1, wanted + 1), own)
    own_ref[...] = own.astype(jnp.float32)
    for total in sums:
        total[...] = jnp.zeros_like(total)


def make_index(by_xor, slabs, cols, fine_columns, fine_counts, coarse_pattern):
    bricks = fine_counts.shape[0]
    owned = coarse_pattern.shape[1] // cols
    slots = fine_columns.shape[1]
    up = lambda n, to: -(-n // to) * to
    return pl.pallas_call(
        functools.partial(index_kernel, by_xor, slabs, cols),
        out_shape=(
            pltpu.SMEM((1, bricks * slots), jnp.int32),
            pltpu.VMEM((up(slabs * bricks, LANES), LANES), jnp.bfloat16),
            pltpu.VMEM((up(owned, 8), LANES), jnp.float32),
        )
        + (pltpu.VMEM((owned + 1, BRICK, LANES), jnp.float32),) * (bricks * P_SLOTS),
        in_specs=[pl.BlockSpec(memory_space=pltpu.SMEM)] * 3,
        out_specs=(pl.BlockSpec(memory_space=pltpu.SMEM),)
        + (pl.BlockSpec(memory_space=pltpu.VMEM),) * (2 + bricks * P_SLOTS),
        compiler_params=pltpu.CompilerParams(vmem_limit_bytes=SMALL),
        name="index",
    )(fine_columns, fine_counts, coarse_pattern)


def operator_kernel(
    slabs, masks, bricks, slots, owned, start_ref, pick_ref, own_ref, restrict_ref, *refs, cols
):
    parts = len(masks) if masks else 1
    fines, refs = refs[:cols], refs[cols:]
    pieces, refs = refs[:parts], refs[parts:]
    refs = refs[bricks * P_SLOTS :]
    out_ref, refs = refs[0], refs[1:]
    sums, refs = refs[: bricks * P_SLOTS], refs[bricks * P_SLOTS :]
    held_ref, result_ref, out_sem = refs
    share = slots // cols
    rows = bricks * BRICK + EXTRA

    table = [jnp.zeros((EXTRA, LANES), jnp.float32) for _ in range(pick_ref.shape[0] // LANES)]
    for piece, inside in zip(pieces, masks if masks else [range(slabs)]):
        for at, slab in enumerate(inside):
            first = at * rows + bricks * BRICK
            digits = piece[first : first + EXTRA, :].astype(jnp.float32)
            tile, shift = slab * bricks // LANES, slab * bricks % LANES
            table[tile] += pltpu.roll(digits, shift, 1) if shift else digits
    reached = jnp.dot(
        jnp.concatenate(table, axis=1).astype(jnp.bfloat16),
        pick_ref[...],
        preferred_element_type=jnp.float32,
    )
    own = own_ref[...]
    found = []
    offset = lax.broadcasted_iota(jnp.int32, own.shape, 0).astype(jnp.float32) - owned
    for q in range(P_SLOTS):
        coarse = reached[2 * q : 2 * q + 1, :] + DIGIT * reached[2 * q + 1 : 2 * q + 2, :]
        slot = owned + jnp.sum(jnp.where(own == coarse, offset, 0.0), axis=0, keepdims=True)
        found.append(slot.astype(jnp.int32))
    goals = found[0] + GOAL * found[1]

    source = pieces[0]
    if masks:
        source = held_ref
        for piece, inside in zip(pieces, masks):
            for at, slab in enumerate(inside):
                held_ref[slab * rows : (slab + 1) * rows, :] = piece[at * rows : (at + 1) * rows, :]
    left = lax.broadcasted_iota(jnp.int32, (BRICK, LANES), 1) < BRICK
    nothing = jnp.zeros((BRICK, LANES), jnp.bfloat16)

    for part in range(cols):
        for pair in range(share // 2):
            for i in range(bricks):
                blocks, where_to = [], []
                for half in range(2):
                    at = i * slots + part * share + pair * 2 + half
                    start = pl.multiple_of(start_ref[0, at], 16)
                    blocks.append(source[pl.ds(start, BRICK), :])
                    goal = goals[0, at]
                    where_to += [goal & (GOAL - 1), goal >> GOAL_BITS]
                right = jnp.concatenate(
                    [
                        jnp.concatenate([blocks[0], nothing], axis=1),
                        jnp.concatenate([nothing, blocks[1]], axis=1),
                    ],
                    axis=0,
                )
                a = fines[part][i * BRICK : (i + 1) * BRICK, pair * LANES : (pair + 1) * LANES]
                product = jnp.dot(a, right, preferred_element_type=jnp.float32)
                for half in range(2):
                    block = product[:, half * LANES : (half + 1) * LANES]
                    for q in range(P_SLOTS):
                        sums[i * P_SLOTS + q][where_to[half * P_SLOTS + q]] += block

    restrict = restrict_ref[...]
    leaving = []
    for at in range(owned // 2):
        high, low = [], []
        for i in range(bricks):
            even, odd = (
                [sums[i * P_SLOTS + q][2 * at + side] for q in range(P_SLOTS)] for side in range(2)
            )
            total = jnp.where(left, even[0], odd[1]) + pltpu.roll(
                jnp.where(left, odd[0], even[1]), BRICK, 1
            )
            high.append(total.astype(jnp.bfloat16))
            low.append((total - high[-1].astype(jnp.float32)).astype(jnp.bfloat16))
        high = jnp.concatenate(high, axis=0)
        low = jnp.concatenate(low, axis=0)
        here = pl.ds(at * LANES, LANES)
        result_ref[:, here] = jnp.dot(restrict, high, preferred_element_type=jnp.float32) + jnp.dot(
            restrict, low, preferred_element_type=jnp.float32
        )
        move = pltpu.make_async_copy(result_ref.at[:, here], out_ref.at[:, here], out_sem.at[at])
        move.start()
        leaving.append(move)
    for move in leaving:
        move.wait()


def operate(slabs, cols, bricks, slots, owned, index, restrict_rows, fines, pieces, masks):
    rows = bricks * BRICK + EXTRA
    vmem = pl.BlockSpec(memory_space=pltpu.VMEM)
    smem = pl.BlockSpec(memory_space=pltpu.SMEM)
    held_rows = slabs * rows if masks else 16
    shape = (restrict_rows.shape[0], owned * BRICK)
    starts, pick, own, *sums = index
    starts = pltpu.with_memory_space_constraint(starts, pltpu.SMEM)
    given = (starts, pick, own, restrict_rows, *fines, *pieces)
    return pl.pallas_call(
        functools.partial(operator_kernel, slabs, masks, bricks, slots, owned, cols=cols),
        out_shape=[jax.ShapeDtypeStruct(shape, jnp.float32)]
        + [pltpu.VMEM(each.shape, jnp.float32) for each in sums],
        in_specs=[smem] + [vmem] * (len(given) - 1 + len(sums)),
        out_specs=[pl.BlockSpec(memory_space=pl.ANY)] + [vmem] * len(sums),
        input_output_aliases={len(given) + at: 1 + at for at in range(len(sums))},
        scratch_shapes=[
            pltpu.VMEM((held_rows, LANES), jnp.bfloat16),
            pltpu.VMEM(shape, jnp.float32),
            pltpu.SemaphoreType.DMA((owned // 2,)),
        ],
        compiler_params=pltpu.CompilerParams(vmem_limit_bytes=32 * 1024 * 1024),
        name="operator",
    )(*given, *sums)[0]


def local(
    slabs,
    cols,
    fine_matrix,
    fine_columns,
    fine_counts,
    prolong,
    prolong_columns,
    restrict_rows,
    coarse_pattern,
):
    bricks, slots = fine_columns.shape
    owned = coarse_pattern.shape[1] // cols
    packed = pack(prolong, prolong_columns)
    others = [swap(fine_matrix, "col", cols, d) for d in range(1, cols)]

    def make(after):
        columns, _ = lax.optimization_barrier((fine_columns, after))
        return make_index(slabs == 16, slabs, cols, columns, fine_counts, coarse_pattern)

    pieces, masks, index = gather_row(packed, slabs, make)
    fines = [pltpu.with_memory_space_constraint(fine_matrix, pltpu.VMEM)] + others
    return operate(slabs, cols, bricks, slots, owned, index, restrict_rows, fines, pieces, masks)


def solution(mesh):
    return jax.shard_map(
        functools.partial(local, mesh.shape["row"], mesh.shape["col"]),
        mesh=mesh,
        in_specs=(
            P("row", "col"),
            P("row", None),
            P("row"),
            P("row", None),
            P("row", None),
            P("row", None),
            P("row", None),
        ),
        out_specs=P("row", "col"),
        check_vma=False,
    )
```

```python
import functools

import jax
import jax.numpy as jnp
from jax import lax
from jax.experimental import pallas as pl
from jax.experimental.pallas import tpu as pltpu
from jax.sharding import PartitionSpec as P

BRICK = 64
P_SLOTS = 2
DIGIT = 128
LANES = 128
EXTRA = 16
GOAL_BITS = 8
GOAL = 1 << GOAL_BITS
SMALL = 8 * 1024 * 1024
LIMIT = 32 * 1024 * 1024
LATE = 1


def pack_kernel(columns_ref, prolong_ref, packed_ref):
    rows = prolong_ref.shape[0]
    packed_ref[:rows, :] = prolong_ref[...]
    row = lax.broadcasted_iota(jnp.int32, (EXTRA, LANES), 0)
    lane = lax.broadcasted_iota(jnp.int32, (EXTRA, LANES), 1)
    digits = jnp.zeros((EXTRA, LANES), jnp.int32)
    for brick in range(columns_ref.shape[1]):
        for q in range(P_SLOTS):
            value = columns_ref[q, brick] + 1
            here = lane == brick
            digits = jnp.where(here & (row == 2 * q), lax.rem(value, DIGIT), digits)
            digits = jnp.where(here & (row == 2 * q + 1), lax.div(value, DIGIT), digits)
    packed_ref[rows:, :] = digits.astype(jnp.float32).astype(jnp.bfloat16)


def pack(prolong, prolong_columns):
    return pl.pallas_call(
        pack_kernel,
        out_shape=pltpu.VMEM((prolong.shape[0] + EXTRA, LANES), jnp.bfloat16),
        in_specs=[
            pl.BlockSpec(memory_space=pltpu.SMEM),
            pl.BlockSpec(memory_space=pltpu.VMEM),
        ],
        out_specs=pl.BlockSpec(memory_space=pltpu.VMEM),
        name="pack",
    )(prolong_columns.T, prolong)


def swap(block, axis, size, mask):
    return lax.ppermute(block, axis, [(i, i ^ mask) for i in range(size)])


def gather_row(packed, size, make):
    if size != 16:
        return [lax.all_gather(packed, "row", axis=0, tiled=True)], None, make(packed)
    got = {(0,): packed}
    for mask in (8, 12, 4):
        got[(mask,)] = swap(packed, "row", size, mask)
    across = {}
    for group in ((12,), (0,), (4,), (8,)):
        both = jnp.concatenate([got[(mask,)] for mask in group])
        across[tuple(mask | 2 for mask in group)] = swap(both, "row", size, 2)
    index = list(make(got[(8,)]))
    pieces = {**got, **across}
    for half in (((0,), (8,), (4,), (12,)), ((6,), (14,), (2,), (10,))):
        both = jnp.concatenate([pieces[inside] for inside in half])
        if half[0] in across:
            both, index[1] = lax.optimization_barrier((both, index[1]))
        group = tuple(mask | 1 for inside in half for mask in inside)
        pieces[group] = swap(both, "row", size, 1)
    return list(pieces.values()), list(pieces), index


def index_kernel(
    by_xor, slabs, cols, columns_ref, counts_ref, pattern_ref, start_ref, pick_ref, own_ref, *sums
):
    bricks, slots = columns_ref.shape
    share = slots // cols
    owned = pattern_ref.shape[1] // cols
    rows = bricks * BRICK + EXTRA
    row_index = lax.axis_index("row")
    col_index = lax.axis_index("col")
    lane = lax.broadcasted_iota(jnp.int32, (8, LANES), 1)
    slab_of = jnp.zeros((8, LANES), jnp.int32)
    inner_of = jnp.zeros((8, LANES), jnp.int32)
    live_of = jnp.zeros((8, LANES), jnp.int32)
    for i in range(bricks):
        for part in range(cols):
            first = (col_index ^ part) * share if cols > 1 else 0
            for pos in range(share):
                brick = columns_ref[i, first + pos]
                slab = lax.div(brick, bricks)
                inner = brick - slab * bricks
                if by_xor:
                    slab = slab ^ row_index
                start_ref[0, i * slots + part * share + pos] = slab * rows + inner * BRICK
                here = lane == i * slots + part * share + pos
                slab_of = jnp.where(here, slab, slab_of)
                inner_of = jnp.where(here, inner, inner_of)
                live_of = jnp.where(here, (first + pos < counts_ref[i]).astype(jnp.int32), live_of)
    place = jnp.where(live_of == 1, slab_of * bricks + inner_of, -1)[0:1, :]
    row = lax.broadcasted_iota(jnp.int32, pick_ref.shape, 0)
    pick_ref[...] = (row == place).astype(jnp.float32).astype(jnp.bfloat16)
    own = jnp.full(own_ref.shape, -1, jnp.int32)
    row = lax.broadcasted_iota(jnp.int32, own_ref.shape, 0)
    for s in range(owned):
        wanted = pattern_ref[0, col_index * owned + s]
        own = jnp.where(row == s, jnp.where(wanted < 0, -1, wanted + 1), own)
    own_ref[...] = own.astype(jnp.float32)
    for total in sums:
        total[...] = jnp.zeros_like(total)


def make_index(by_xor, slabs, cols, fine_columns, fine_counts, coarse_pattern):
    bricks = fine_counts.shape[0]
    owned = coarse_pattern.shape[1] // cols
    slots = fine_columns.shape[1]
    up = lambda n, to: -(-n // to) * to
    return pl.pallas_call(
        functools.partial(index_kernel, by_xor, slabs, cols),
        out_shape=(
            pltpu.SMEM((1, bricks * slots), jnp.int32),
            pltpu.VMEM((up(slabs * bricks, LANES), LANES), jnp.bfloat16),
            pltpu.VMEM((up(owned, 8), LANES), jnp.float32),
        )
        + (pltpu.VMEM((owned + 1, BRICK, LANES), jnp.float32),) * (bricks * P_SLOTS),
        in_specs=[pl.BlockSpec(memory_space=pltpu.SMEM)] * 3,
        out_specs=(pl.BlockSpec(memory_space=pltpu.SMEM),)
        + (pl.BlockSpec(memory_space=pltpu.VMEM),) * (2 + bricks * P_SLOTS),
        compiler_params=pltpu.CompilerParams(vmem_limit_bytes=SMALL),
        name="index",
    )(*(pltpu.with_memory_space_constraint(each, pltpu.HBM) for each in (fine_columns, fine_counts, coarse_pattern)))


def take_in(piece, inside, bricks, table, held_ref):
    rows = bricks * BRICK + EXTRA
    for at, slab in enumerate(inside):
        block = piece[at * rows : (at + 1) * rows, :]
        if held_ref is not None:
            held_ref[slab * rows : (slab + 1) * rows, :] = block
        digits = block[bricks * BRICK :, :].astype(jnp.float32)
        tile, shift = slab * bricks // LANES, slab * bricks % LANES
        table[tile] += pltpu.roll(digits, shift, 1) if shift else digits


def prep_kernel(masks, bricks, *refs):
    pieces, (held_ref, table_ref) = refs[:-2], refs[-2:]
    table = [jnp.zeros((EXTRA, LANES), jnp.float32)]
    for piece, inside in zip(pieces, masks):
        take_in(piece, inside, bricks, table, held_ref)
    table_ref[...] = table[0]


def make_prep(slabs, bricks, pieces, masks):
    vmem = pl.BlockSpec(memory_space=pltpu.VMEM)
    return pl.pallas_call(
        functools.partial(prep_kernel, masks, bricks),
        out_shape=[
            pltpu.VMEM((slabs * (bricks * BRICK + EXTRA), LANES), jnp.bfloat16),
            pltpu.VMEM((EXTRA, LANES), jnp.float32),
        ],
        in_specs=[vmem] * len(pieces),
        out_specs=[vmem] * 2,
        compiler_params=pltpu.CompilerParams(vmem_limit_bytes=LIMIT),
        name="prep",
    )(*pieces)


def operator_kernel(
    slabs, masks, bricks, slots, owned, start_ref, pick_ref, own_ref, restrict_ref, *refs, cols
):
    late = len(masks) if masks else 1
    fines, refs = refs[:cols], refs[cols:]
    given, refs = refs[:late], refs[late:]
    kept = bricks * P_SLOTS
    share = slots // cols
    if masks:
        table_ref, refs = refs[0], refs[2 + kept :]
        out_ref, source, *refs = refs
        table = [table_ref[...]]
        for piece, inside in zip(given, masks):
            take_in(piece, inside, bricks, table, source)
    else:
        out_ref, *refs = refs[kept:]
        source = given[0]
        table = [jnp.zeros((EXTRA, LANES), jnp.float32) for _ in range(pick_ref.shape[0] // LANES)]
        take_in(source, range(slabs), bricks, table, None)
    sums, (result_ref, out_sem) = refs[:kept], refs[kept:]

    reached = jnp.dot(
        jnp.concatenate(table, axis=1).astype(jnp.bfloat16),
        pick_ref[...],
        preferred_element_type=jnp.float32,
    )
    own = own_ref[...]
    found = []
    offset = lax.broadcasted_iota(jnp.int32, own.shape, 0).astype(jnp.float32) - owned
    for q in range(P_SLOTS):
        coarse = reached[2 * q : 2 * q + 1, :] + DIGIT * reached[2 * q + 1 : 2 * q + 2, :]
        slot = owned + jnp.sum(jnp.where(own == coarse, offset, 0.0), axis=0, keepdims=True)
        found.append(slot.astype(jnp.int32))
    goals = found[0] + GOAL * found[1]

    left = lax.broadcasted_iota(jnp.int32, (BRICK, LANES), 1) < BRICK
    nothing = jnp.zeros((BRICK, LANES), jnp.bfloat16)

    for part in range(cols):
        for pair in range(share // 2):
            for i in range(bricks):
                blocks, where_to = [], []
                for half in range(2):
                    at = i * slots + part * share + pair * 2 + half
                    start = pl.multiple_of(start_ref[0, at], 16)
                    blocks.append(source[pl.ds(start, BRICK), :])
                    goal = goals[0, at]
                    where_to += [goal & (GOAL - 1), goal >> GOAL_BITS]
                right = jnp.concatenate(
                    [
                        jnp.concatenate([blocks[0], nothing], axis=1),
                        jnp.concatenate([nothing, blocks[1]], axis=1),
                    ],
                    axis=0,
                )
                a = fines[part][i * BRICK : (i + 1) * BRICK, pair * LANES : (pair + 1) * LANES]
                product = jnp.dot(a, right, preferred_element_type=jnp.float32)
                for half in range(2):
                    block = product[:, half * LANES : (half + 1) * LANES]
                    for q in range(P_SLOTS):
                        sums[i * P_SLOTS + q][where_to[half * P_SLOTS + q]] += block

    restrict = restrict_ref[...]
    leaving = []
    for at in range(owned // 2):
        high, low = [], []
        for i in range(bricks):
            even, odd = (
                [sums[i * P_SLOTS + q][2 * at + side] for q in range(P_SLOTS)] for side in range(2)
            )
            total = jnp.where(left, even[0], odd[1]) + pltpu.roll(
                jnp.where(left, odd[0], even[1]), BRICK, 1
            )
            high.append(total.astype(jnp.bfloat16))
            low.append((total - high[-1].astype(jnp.float32)).astype(jnp.bfloat16))
        high = jnp.concatenate(high, axis=0)
        low = jnp.concatenate(low, axis=0)
        here = pl.ds(at * LANES, LANES)
        result_ref[:, here] = jnp.dot(restrict, high, preferred_element_type=jnp.float32) + jnp.dot(
            restrict, low, preferred_element_type=jnp.float32
        )
        move = pltpu.make_async_copy(result_ref.at[:, here], out_ref.at[:, here], out_sem.at[at])
        move.start()
        leaving.append(move)
    for move in leaving:
        move.wait()


def operate(slabs, cols, bricks, slots, owned, index, restrict_rows, fines, pieces, masks):
    vmem = pl.BlockSpec(memory_space=pltpu.VMEM)
    smem = pl.BlockSpec(memory_space=pltpu.SMEM)
    shape = (restrict_rows.shape[0], owned * BRICK)
    starts, pick, own, *kept = index
    starts = pltpu.with_memory_space_constraint(starts, pltpu.SMEM)
    given = [starts, pick, own, restrict_rows, *fines, *pieces[-LATE:]]
    if masks:
        held, table = make_prep(slabs, bricks, pieces[:-LATE], masks[:-LATE])
        given.append(table)
        kept = [held] + kept
    return pl.pallas_call(
        functools.partial(
            operator_kernel, slabs, masks[-LATE:] if masks else None, bricks, slots, owned, cols=cols
        ),
        out_shape=[jax.ShapeDtypeStruct(shape, jnp.float32)]
        + [pltpu.VMEM(each.shape, each.dtype) for each in kept],
        in_specs=[smem] + [vmem] * (len(given) - 1 + len(kept)),
        out_specs=[pl.BlockSpec(memory_space=pl.ANY)] + [vmem] * len(kept),
        input_output_aliases={len(given) + at: 1 + at for at in range(len(kept))},
        scratch_shapes=[
            pltpu.VMEM(shape, jnp.float32),
            pltpu.SemaphoreType.DMA((owned // 2,)),
        ],
        compiler_params=pltpu.CompilerParams(vmem_limit_bytes=LIMIT),
        name="operator",
    )(*given, *kept)[0]


def local(
    slabs,
    cols,
    fine_matrix,
    fine_columns,
    fine_counts,
    prolong,
    prolong_columns,
    restrict_rows,
    coarse_pattern,
):
    bricks, slots = fine_columns.shape
    owned = coarse_pattern.shape[1] // cols
    packed = pack(prolong, prolong_columns)
    others = [swap(fine_matrix, "col", cols, d) for d in range(1, cols)]

    def make(after):
        columns, _ = lax.optimization_barrier((fine_columns, after))
        return make_index(slabs == 16, slabs, cols, columns, fine_counts, coarse_pattern)

    pieces, masks, index = gather_row(packed, slabs, make)
    fines = [pltpu.with_memory_space_constraint(fine_matrix, pltpu.VMEM)] + others
    return operate(slabs, cols, bricks, slots, owned, index, restrict_rows, fines, pieces, masks)


def solution(mesh):
    return jax.shard_map(
        functools.partial(local, mesh.shape["row"], mesh.shape["col"]),
        mesh=mesh,
        in_specs=(
            P("row", "col"),
            P("row", None),
            P("row"),
            P("row", None),
            P("row", None),
            P("row", None),
            P("row", None),
        ),
        out_specs=P("row", "col"),
        check_vma=False,
    )
```
